32 devices in a mesh: front: 8 (over z, y), sect: 4 (over x, core).
Axes of the slice: x: 2, y: 2, z: 4, core: 2. Of those that a mesh axis runs over, the one named last changes fastest.
Arguments:
- pivot_rows: float32 [8, 4, 512, 512], P('front', 'sect'), may hold values from -6 to 6
- sections: float32 [8, 4, 4, 256, 512], P('front', 'sect'), may hold values from -6 to 6
- sect_vectors: bfloat16 [8, 4, 4, 256, 512], P('front', 'sect'), may hold values from -0.375 to 0.375
- sect_factors: bfloat16 [8, 4, 4, 512, 512], P('front', 'sect'), may hold values from -0.125 to 0.125
- routes: int32 [8, 4, 1024, 1], P('front', 'sect'), may hold values from 0 to 7; in each aligned block of 1024 rows (0 to 1023, 1024 to 2047, ..., all dimensions but the last counted through in order) at most 192 rows name the same one
- parent_vectors: bfloat16 [8, 4, 1536, 512], P('front', 'sect'), may hold values from -0.078125 to 0.078125
- parent_factor: bfloat16 [8, 512, 512], P('front'), may hold values from -0.25 to 0.25
Outputs:
- top_rows: float32 [8, 4, 512, 512], P('front', 'sect')
- parent_rows: float32 [8, 4, 1536, 512], P('front', 'sect')
The draws below stay inside these ranges and needn't reach their ends.
Inputs may be any that keep to these rules, and one draw needn't show every extreme that they name: `routes`: the rows of one section name each parent owner at most 192 times, a bound that some block reaches.
All inputs are finite; a program needn't handle non-finite values.
Results may differ from the reference program's by a relative error of at most 0.0003.
Values sent between devices are 32-bit elements; how exact they have to be, the bound alone decides.
A program may use at most 128 MiB of HBM per device.

```python
import math
import jax
import jax.numpy as jnp
import numpy as np
from jax import lax

NRHS = 512
PW = 512
SEC = 256
PANELS = 4
FRONTS = 8
ROWS_DEV = 1024
CAPS = 192
PROWS = 1536
N_FRONT = 8
N_SECT = 4


def shard_levels(key, dims, split, smallest, high):
    def one(position, shards_of):
        draws = jax.random.uniform(jax.random.fold_in(jax.random.fold_in(key, 6), position), (shards_of,), jnp.float32, smallest / len(split), high / len(split))
        return jnp.repeat(jnp.exp(draws), dims[position] // shards_of).reshape((-1,) + (1,) * (len(dims) - position - 1))

    loudness = one(*split[0])
    for cut in split[1:]:
        loudness = loudness * one(*cut)
    return loudness


def routed_block(own_key, own, number, rows, number_of, top, limit, skew):
    sequence = jax.random.permutation(own_key, number_of)
    packed, ordinary = shares(number_of, rows * top, limit, skew, True), shares(number_of, rows * top, limit, skew, False)
    places = jnp.arange(number_of)

    def named(lengths, offset_by):
        used = int((lengths > 0).sum())
        fixed = max(1, used // 4)
        shifted = fixed + (places - fixed + offset_by * (used - fixed)) % max(1, number_of - fixed)
        return jnp.zeros((number_of,), jnp.int32).at[sequence[jnp.where(places < fixed, places, shifted)]].set(jnp.asarray(lengths, jnp.int32))

    lengths = jnp.where(number % 4 == 0, named(packed, number // 4), named(ordinary, number - number // 4 - 1))
    mixed = jax.random.permutation(jax.random.fold_in(own, 3), number_of)
    source_of, receiver = mixed[0:number_of // 2 * 2:2], mixed[1:number_of // 2 * 2:2]
    slack = jnp.minimum(lengths[source_of] - 1, limit - lengths[receiver]) // 2
    slack = jnp.where((source_of == sequence[0]) | (receiver == sequence[0]) | (lengths[receiver] == 0), 0, jnp.maximum(slack, 0))
    shifted = jax.random.randint(jax.random.fold_in(own, 4), (number_of // 2,), 0, 1 << 20) % (slack + 1)
    lengths = lengths.at[source_of].add(-shifted).at[receiver].add(shifted)
    members = jnp.searchsorted(jnp.cumsum(lengths), jnp.arange(rows * top), side="right").astype(jnp.int32)
    table = members.reshape(top, rows).T
    table = table[jax.random.permutation(jax.random.fold_in(own, 1), rows)]
    offset_by = jax.random.randint(jax.random.fold_in(own, 2), (rows, 1), 0, top)
    return jnp.take_along_axis(table, (jnp.arange(top)[None, :] + offset_by) % top, axis=1)


def shares(number_of, total, most, lean, full):
    weights = [(1 << 20) // math.isqrt(grade ** lean) + 1 for grade in range(1, number_of + 1)]
    largest = most if full else min(most, max(-(-total // number_of), total * weights[0] // sum(weights)))
    least = 1 if total - largest >= number_of - 1 else 0
    given, rest = [largest] + [least] * (number_of - 1), total - largest - least * (number_of - 1)
    while rest > 0:
        candidates = [i for i in range(1, number_of) if given[i] < largest] or [i for i in range(1, number_of) if given[i] < most]
        mass, remaining = sum([weights[i] for i in candidates]), rest
        for i in candidates:
            more = min(most - given[i], max(1, remaining * weights[i] // mass), rest)
            given[i] = given[i] + more
            rest = rest - more
    return np.array(given)


def bell_draw(own_key, dims, scale, reach, split=(), kind=jnp.bfloat16):
    values = jax.random.normal(own_key, dims, jnp.float32) * scale
    if len(split) > 0:
        values = shard_levels(own_key, dims, split, -0.22, 0.18) * values
    return jnp.clip(values, min=-reach, max=reach).astype(kind)


def setup_inputs(seed: int = 0) -> dict:
    splits = jax.random.split(jax.random.key(seed), 8)
    pivot_rows = bell_draw(splits[0], (FRONTS, PANELS, PW, NRHS), 1.0, 6.0, ((0, 8), (1, 4)), jnp.float32)
    sections = bell_draw(splits[1], (FRONTS, N_SECT, PANELS, SEC, NRHS), 1.0, 6.0, ((0, 8), (1, 4)), jnp.float32)
    sect_vectors = bell_draw(splits[2], (FRONTS, N_SECT, PANELS, SEC, PW), SEC ** -0.5, 0.375, ((0, 8), (1, 4)))
    sect_factors = bell_draw(splits[3], (FRONTS, N_SECT, PANELS, PW, PW), (4 * PW) ** -0.5, 0.125, ((0, 8), (1, 4)))
    routes_keys = jax.random.split(jax.random.fold_in(splits[4], 1), FRONTS * N_SECT * ROWS_DEV // ROWS_DEV)
    routes_turns = jax.random.permutation(jax.random.fold_in(splits[4], 3), FRONTS * N_SECT * ROWS_DEV // ROWS_DEV)
    routes = jax.vmap(lambda own, number: routed_block(jax.random.fold_in(splits[4], 2), own, number, ROWS_DEV, N_FRONT, 1, CAPS, 2))(routes_keys, routes_turns).reshape((FRONTS, N_SECT, ROWS_DEV, 1))
    parent_vectors = bell_draw(splits[5], (FRONTS, N_SECT, PROWS, PW), (N_SECT * PROWS) ** -0.5, 0.078125, ((0, 8), (1, 4)))
    parent_factor = bell_draw(splits[6], (FRONTS, PW, PW), PW ** -0.5, 0.25, ((0, 8),))
    return {"pivot_rows": pivot_rows, "sections": sections, "sect_vectors": sect_vectors, "sect_factors": sect_factors, "routes": routes, "parent_vectors": parent_vectors, "parent_factor": parent_factor}


highest = lax.Precision.HIGHEST


def reflect(pivot_block, row_block, vectors, factor):
    vectors = vectors.astype(jnp.float32)
    factor = factor.astype(jnp.float32)
    inner_sum = pivot_block + jnp.einsum('rp,rn->pn', vectors, row_block, precision=highest)
    change = jnp.einsum('qp,qn->pn', factor, inner_sum, precision=highest)
    return pivot_block - change, row_block - jnp.dot(vectors, change, precision=highest)


def front_chain(carried):
    pivots, blocks, vectors, factors = carried
    finished = []
    for panel_id in range(PANELS):
        pivot_block = pivots[panel_id]
        for step_id in range(N_SECT):
            owner_id = (panel_id + step_id) % N_SECT
            pivot_block, updated = reflect(pivot_block, blocks[owner_id, panel_id], vectors[owner_id, panel_id], factors[owner_id, panel_id])
            blocks = blocks.at[owner_id, panel_id].set(updated)
        finished.append(pivot_block)
    return jnp.stack(finished), blocks


def reference(pivot_rows, sections, sect_vectors, sect_factors, routes, parent_vectors, parent_factor):
    top_rows, updated = lax.map(front_chain, (pivot_rows, sections, sect_vectors, sect_factors))
    assembled = []
    projection = jnp.zeros((FRONTS, PW, NRHS), jnp.float32)
    for owner_id in range(N_SECT):
        contrib = updated[:, owner_id].reshape(FRONTS, ROWS_DEV, NRHS)
        destination = routes[:, owner_id, :, 0].astype(jnp.int32)
        onehot = (destination[:, :, None] == jnp.arange(FRONTS, dtype=jnp.int32)[None, None, :]).astype(jnp.int32)
        rank_slot = jnp.sum(jnp.cumsum(onehot, axis=1) * onehot, axis=2) - 1
        column_slot = (jnp.arange(FRONTS, dtype=jnp.int32)[:, None] * CAPS + rank_slot).astype(jnp.int32)
        parent = jnp.zeros((FRONTS, PROWS, NRHS), jnp.float32).at[destination, column_slot].set(contrib)
        assembled.append(parent)
        vectors = parent_vectors[:, owner_id].astype(jnp.float32)
        projection = projection + jnp.einsum('frp,frn->fpn', vectors, parent, precision=highest)
    change = jnp.einsum('fqp,fqn->fpn', parent_factor.astype(jnp.float32), projection, precision=highest)
    results = []
    for owner_id in range(N_SECT):
        vectors = parent_vectors[:, owner_id].astype(jnp.float32)
        results.append(assembled[owner_id] - jnp.einsum('frp,fpn->frn', vectors, change, precision=highest))
    return top_rows, jnp.stack(results, axis=1)
```

```python
import jax
import jax.numpy as jnp
from jax import lax
from jax.sharding import PartitionSpec as P

highest = lax.Precision.HIGHEST


def passed_along(value, axis, steps):
    count = lax.axis_size(axis)
    pairs = [(source, (source + steps) % count) for source in range(count)]
    return lax.ppermute(value, axis, pairs)


def reflect(pivot_block, row_block, vectors, factor):
    vectors = vectors.astype(jnp.float32)
    factor = factor.astype(jnp.float32)
    inner_sum = pivot_block + jnp.einsum("rp,rn->pn", vectors, row_block, precision=highest)
    change = jnp.einsum("qp,qn->pn", factor, inner_sum, precision=highest)
    return (pivot_block - change, row_block - jnp.dot(vectors, change, precision=highest))


CHUNKS = 2


def halved_sum(value, axis):
    count = lax.axis_size(axis)
    me = lax.axis_index(axis)
    if count != 4:
        return lax.psum(value, axis)
    near = [(i, i ^ 1) for i in range(count)]
    far = [(i, i ^ 2) for i in range(count)]
    half = value.shape[0] // 2
    odd = me % 2
    mine = lax.dynamic_slice_in_dim(value, odd * half, half, 0)
    other = lax.dynamic_slice_in_dim(value, (1 - odd) * half, half, 0)
    mine = mine + lax.ppermute(other, axis, near)
    mine = mine + lax.ppermute(mine, axis, far)
    other = lax.ppermute(mine, axis, near)
    low = jnp.where(odd == 0, mine, other)
    high = jnp.where(odd == 0, other, mine)
    return jnp.concatenate([low, high], axis=0)


def local(pivot_rows, sections, sect_vectors, sect_factors, routes, parent_vectors, parent_factor):
    owner_index = lax.axis_index("sect")
    owners_sect = lax.axis_size("sect")
    owners = lax.axis_size("front")
    panels, rows, columns = sections.shape[2:]
    row_count = panels * rows
    capacity = 3 * row_count // (2 * owners)
    destination = routes[0, 0, :, 0]
    onehot = (destination[:, None] == jnp.arange(owners, dtype=jnp.int32)[None, :]).astype(
        jnp.int32
    )
    rank_slot = jnp.sum(jnp.cumsum(onehot, axis=0) * onehot, axis=1) - 1
    slot_index = destination * capacity + rank_slot
    order = [(owner_index - step_id) % owners_sect for step_id in range(owners_sect)]
    vectors = [lax.dynamic_index_in_dim(sect_vectors[0, 0], k, 0, keepdims=False) for k in order]
    factors = [lax.dynamic_index_in_dim(sect_factors[0, 0], k, 0, keepdims=False) for k in order]
    slots = slot_index.reshape(panels, rows)
    slots = jnp.concatenate(
        [lax.dynamic_index_in_dim(slots, k, 0, keepdims=False) for k in order], axis=0
    )
    parent_vec = parent_vectors[0, 0].astype(jnp.float32)
    parent_fac = parent_factor[0].astype(jnp.float32)
    width = columns // CHUNKS
    tops, results = [], []
    for chunk in range(CHUNKS):
        cut = slice(chunk * width, (chunk + 1) * width)
        pivot_block = pivot_rows[0, 0, :, cut]
        pieces = []
        for step_id in range(owners_sect):
            row_block = lax.dynamic_index_in_dim(
                sections[0, 0, :, :, cut], order[step_id], 0, keepdims=False
            )
            pivot_block, updated = reflect(
                pivot_block, row_block, vectors[step_id], factors[step_id]
            )
            pieces.append(updated)
            pivot_block = passed_along(pivot_block, "sect", 1)
        contrib = jnp.concatenate(pieces, axis=0)
        buffer = jnp.zeros((owners * capacity, width), jnp.float32).at[slots].set(contrib)
        buffer = buffer.reshape(owners, capacity, width)
        arrived = lax.all_to_all(
            buffer, "front", split_axis=0, concat_axis=0, tiled=True
        ).reshape(owners * capacity, width)
        partial_value = jnp.einsum("rp,rn->pn", parent_vec, arrived, precision=highest)
        summed = halved_sum(partial_value, "sect")
        change = jnp.einsum("qp,qn->pn", parent_fac, summed, precision=highest)
        results.append(arrived - jnp.dot(parent_vec, change, precision=highest))
        tops.append(pivot_block)
    top = jnp.concatenate(tops, axis=1)
    result = jnp.concatenate(results, axis=1)
    return (top[None, None], result[None, None])


def solution(mesh):
    in_specs = (
        P("front", "sect", None, None),
        P("front", "sect", None, None, None),
        P("front", "sect", None, None, None),
        P("front", "sect", None, None, None),
        P("front", "sect", None, None),
        P("front", "sect", None, None),
        P("front", None, None),
    )
    out_specs = (P("front", "sect", None, None), P("front", "sect", None, None))
    return jax.shard_map(local, mesh=mesh, in_specs=in_specs, out_specs=out_specs, check_vma=False)
```

```python
import functools

import jax
import jax.numpy as jnp
from jax import lax
from jax.experimental import pallas as pl
from jax.experimental.pallas import tpu as pltpu
from jax.sharding import PartitionSpec as P

MESH = pl.DeviceIdType.MESH
WIDTH = 128
TILE = 256
F32 = jnp.float32
BF16 = jnp.bfloat16


def halves(value):
    high = value.astype(BF16)
    low = (value - high.astype(F32)).astype(BF16)
    return jnp.concatenate([high, low], axis=1)


def joined(value):
    return value[:, :WIDTH] + value[:, WIDTH:]


def dot(left, right):
    return joined(jnp.dot(left, right, preferred_element_type=F32))


def dot_t(left, right):
    return joined(
        lax.dot_general(left, right, (((0,), (0,)), ((), ())), preferred_element_type=F32)
    )


def kernel(
    owners, steps, chunks,
    pivot_ref, sect_ref, y_ref, t_ref, route_ref, v_ref, f_ref,
    top_ref, out_ref,
    place, slot_row, pivots, pivots_out, contrib, send, arrived, arrived_cat,
    vt, ft, part, part_near, pair, pair_far, total,
    chain_send, chain_recv, swap_send, swap_recv, sum_send, sum_recv,
):
    front = lax.axis_index("front")
    me = lax.axis_index("sect")
    rows = sect_ref.shape[1]
    row_count = sect_ref.shape[0] * rows
    slots = v_ref.shape[0]
    capacity = slots // owners
    depth = pivot_ref.shape[0]
    half = depth // 2
    lag = steps // 2
    odd = lax.rem(me, 2)
    near = me + 1 - 2 * odd
    far = me + 2 - 4 * lax.rem(me // 2, 2)
    right = lax.rem(me + 1, steps)

    def peer(m):
        found = 0
        bit = 1
        while bit < owners:
            found = found + bit * lax.rem(front // bit + m // bit, 2)
            bit *= 2
        return found

    barrier = pltpu.get_barrier_semaphore()

    @pl.loop(1, owners)
    def _(m):
        pl.semaphore_signal(barrier, inc=1, device_id={"front": peer(m)}, device_id_type=MESH)

    for shift in range(1, steps):
        pl.semaphore_signal(
            barrier, inc=1, device_id={"sect": lax.rem(me + shift, steps)}, device_id_type=MESH
        )

    lanes = 128
    before = (
        lax.broadcasted_iota(jnp.int32, (lanes, lanes), 0)
        <= lax.broadcasted_iota(jnp.int32, (lanes, lanes), 1)
    ).astype(F32)
    owner_ids = lax.broadcasted_iota(jnp.int32, (owners, lanes), 0)
    carry = jnp.zeros((owners, 1), F32)
    for group in range(row_count // lanes):
        cut = slice(group * lanes, (group + 1) * lanes)
        named = route_ref[:, cut]
        hit = (owner_ids == named).astype(F32)
        count = jnp.dot(hit, before, preferred_element_type=F32) + carry
        rank = jnp.sum(hit * count, axis=0, keepdims=True) - 1.0
        slot_row[:, cut] = named.astype(F32) * float(capacity) + rank
        carry = carry + jnp.sum(hit, axis=1, keepdims=True)

    @pl.loop(0, slots // TILE)
    def _(tile):
        ids = lax.broadcasted_iota(jnp.int32, (TILE, row_count), 0) + tile * TILE
        hit = ids.astype(F32) == slot_row[...]
        place[pl.ds(pl.multiple_of(tile * TILE, TILE), TILE), :] = hit.astype(F32).astype(BF16)

    pl.semaphore_wait(barrier, owners - 1 + steps - 1)

    def columns(chunk):
        return pl.ds(pl.multiple_of(chunk * WIDTH, WIDTH), WIDTH)

    def chain_copy(chunk, step):
        return pltpu.make_async_remote_copy(
            src_ref=pivots_out.at[chunk * steps + step],
            dst_ref=pivots.at[chunk * steps + step],
            send_sem=chain_send.at[chunk * steps + step],
            recv_sem=chain_recv.at[chunk * steps + step],
            device_id={"sect": right},
            device_id_type=MESH,
        )

    def swap_copy(chunk, m):
        to = peer(m)
        return pltpu.make_async_remote_copy(
            src_ref=send.at[chunk, pl.ds(pl.multiple_of(to * capacity, 8), capacity)],
            dst_ref=arrived.at[chunk, pl.ds(pl.multiple_of(front * capacity, 8), capacity)],
            send_sem=swap_send.at[chunk],
            recv_sem=swap_recv.at[chunk],
            device_id={"front": to},
            device_id_type=MESH,
        )

    def reflect(chunk, step, pivot_block):
        panel = lax.rem(me - step + steps, steps)
        row_block = sect_ref[panel, :, columns(chunk)]
        vectors = y_ref[panel]
        inner = pivot_block + dot_t(vectors, halves(row_block))
        change = dot_t(t_ref[panel], halves(inner))
        pivots_out[chunk * steps + step] = pivot_block - change
        chain_copy(chunk, step).start()
        updated = row_block - dot(vectors, halves(change))
        contrib[chunk, pl.ds(pl.multiple_of(panel * rows, rows), rows), :] = halves(updated)

    def later_step(chunk, step):
        chain_copy(chunk, step - 1).wait_recv()
        reflect(chunk, step, pivots[chunk * steps + step - 1])

    def exchange(chunk):
        @pl.loop(0, slots // TILE)
        def _(tile):
            cut = pl.ds(pl.multiple_of(tile * TILE, TILE), TILE)
            send[chunk, cut, :] = dot(place[cut, :], contrib[chunk])

        @pl.loop(1, owners)
        def _(m):
            swap_copy(chunk, owners - m).start()

        own = pl.ds(pl.multiple_of(front * capacity, 8), capacity)
        arrived[chunk, own, :] = send[chunk, own, :]

    @pl.loop(0, lag * (chunks + 1))
    def _(slot):
        within = lax.rem(slot, lag)

        @pl.when(slot >= lag)
        def _():
            later_step(slot // lag - 1, within + lag)

            @pl.when(within == lag - 1)
            def _():
                exchange(slot // lag - 1)

        @pl.when(slot < lag * chunks)
        def _():
            @pl.when(within == 0)
            def _():
                reflect(slot // lag, 0, pivot_ref[:, columns(slot // lag)])

            @pl.when(within > 0)
            def _():
                later_step(slot // lag, within)

    @pl.loop(0, slots // TILE)
    def _(tile):
        cut = pl.ds(pl.multiple_of(tile * TILE, TILE), TILE)
        vt[:, cut] = v_ref[cut, :].T

    ft[...] = f_ref[...].T

    @pl.loop(0, chunks)
    def _(chunk):
        chain_copy(chunk, steps - 1).wait_recv()
        top_ref[:, columns(chunk)] = pivots[chunk * steps + steps - 1]

    def sum_copy(chunk, stage, source, target, to):
        return pltpu.make_async_remote_copy(
            src_ref=source,
            dst_ref=target,
            send_sem=sum_send.at[chunk * 3 + stage],
            recv_sem=sum_recv.at[chunk * 3 + stage],
            device_id={"sect": to},
            device_id_type=MESH,
        )

    mine = pl.ds(pl.multiple_of(odd * half, half), half)
    other = pl.ds(pl.multiple_of((1 - odd) * half, half), half)

    def sum_copies(chunk):
        return (
            sum_copy(chunk, 0, part.at[chunk, other], part_near.at[chunk], near),
            sum_copy(chunk, 1, pair.at[chunk], pair_far.at[chunk], far),
            sum_copy(chunk, 2, total.at[chunk, mine], total.at[chunk, mine], near),
        )

    def swapped(chunk, sem):
        whole = send.at[chunk, pl.ds(0, (owners - 1) * capacity)]
        return pltpu.make_async_copy(whole, whole, sem.at[chunk])

    @pl.loop(0, chunks)
    def _(chunk):
        swapped(chunk, swap_recv).wait()
        first, second, third = sum_copies(chunk)

        @pl.loop(0, slots // TILE)
        def _(tile):
            cut = pl.ds(pl.multiple_of(tile * TILE, TILE), TILE)
            arrived_cat[cut, :] = halves(arrived[chunk, cut, :])

        part[chunk, other, :] = dot(vt[other, :], arrived_cat[...])
        first.start()
        part[chunk, mine, :] = dot(vt[mine, :], arrived_cat[...])
        first.wait_recv()
        pair[chunk] = part[chunk, mine, :] + part_near[chunk]
        second.start()
        second.wait_recv()
        total[chunk, mine, :] = pair[chunk] + pair_far[chunk]
        third.start()
        third.wait_recv()
        change = halves(dot(ft[...], halves(total[chunk])))

        @pl.loop(0, slots // TILE)
        def _(tile):
            cut = pl.ds(pl.multiple_of(tile * TILE, TILE), TILE)
            out_ref[cut, columns(chunk)] = arrived[chunk, cut, :] - dot(v_ref[cut, :], change)

    @pl.loop(0, chunks)
    def _(chunk):
        for copy in sum_copies(chunk):
            copy.wait_send()
        swapped(chunk, swap_send).wait()

    @pl.loop(0, chunks * steps)
    def _(index):
        chain_copy(index // steps, lax.rem(index, steps)).wait_send()


def local(pivot_rows, sections, sect_vectors, sect_factors, routes, parent_vectors, parent_factor):
    owners = lax.axis_size("front")
    steps = lax.axis_size("sect")
    panels, rows, columns = sections.shape[2:]
    depth = pivot_rows.shape[2]
    slots = parent_vectors.shape[2]
    row_count = panels * rows
    chunks = columns // WIDTH
    half = depth // 2
    vmem = pl.BlockSpec(memory_space=pltpu.VMEM)
    dma = pltpu.SemaphoreType.DMA
    top, result = pl.pallas_call(
        functools.partial(kernel, owners, steps, chunks),
        out_shape=(
            jax.ShapeDtypeStruct((depth, columns), F32),
            jax.ShapeDtypeStruct((slots, columns), F32),
        ),
        in_specs=[vmem] * 7,
        out_specs=(vmem, vmem),
        scratch_shapes=[
            pltpu.VMEM((slots, row_count), BF16),
            pltpu.VMEM((1, row_count), F32),
            pltpu.VMEM((chunks * steps, depth, WIDTH), F32),
            pltpu.VMEM((chunks * steps, depth, WIDTH), F32),
            pltpu.VMEM((chunks, row_count, 2 * WIDTH), BF16),
            pltpu.VMEM((chunks, slots, WIDTH), F32),
            pltpu.VMEM((chunks, slots, WIDTH), F32),
            pltpu.VMEM((slots, 2 * WIDTH), BF16),
            pltpu.VMEM((depth, slots), BF16),
            pltpu.VMEM((depth, depth), BF16),
            pltpu.VMEM((chunks, depth, WIDTH), F32),
            pltpu.VMEM((chunks, half, WIDTH), F32),
            pltpu.VMEM((chunks, half, WIDTH), F32),
            pltpu.VMEM((chunks, half, WIDTH), F32),
            pltpu.VMEM((chunks, depth, WIDTH), F32),
            dma((chunks * steps,)),
            dma((chunks * steps,)),
            dma((chunks,)),
            dma((chunks,)),
            dma((chunks * 3,)),
            dma((chunks * 3,)),
        ],
        compiler_params=pltpu.CompilerParams(
            collective_id=0, has_side_effects=True, vmem_limit_bytes=50 * 2**20
        ),
        cost_estimate=pl.CostEstimate(
            flops=8 * 10**9, bytes_accessed=12 * 2**20, transcendentals=0
        ),
    )(
        pivot_rows[0, 0],
        sections[0, 0],
        sect_vectors[0, 0],
        sect_factors[0, 0],
        routes[0, 0].reshape(1, row_count),
        parent_vectors[0, 0],
        parent_factor[0],
    )
    return (top[None, None], result[None, None])


def solution(mesh):
    in_specs = (
        P("front", "sect", None, None),
        P("front", "sect", None, None, None),
        P("front", "sect", None, None, None),
        P("front", "sect", None, None, None),
        P("front", "sect", None, None),
        P("front", "sect", None, None),
        P("front", None, None),
    )
    out_specs = (P("front", "sect", None, None), P("front", "sect", None, None))
    return jax.shard_map(local, mesh=mesh, in_specs=in_specs, out_specs=out_specs, check_vma=False)
```

```python
import functools

import jax
import jax.numpy as jnp
from jax import lax
from jax.experimental import pallas as pl
from jax.experimental.pallas import tpu as pltpu
from jax.sharding import PartitionSpec as P

MESH = pl.DeviceIdType.MESH
WIDTH = 128
TILE = 256
F32 = jnp.float32
BF16 = jnp.bfloat16


def halves(value):
    high = value.astype(BF16)
    low = (value - high.astype(F32)).astype(BF16)
    return jnp.concatenate([high, low], axis=1)


def joined(value):
    return value[:, :WIDTH] + value[:, WIDTH:]


def dot(left, right):
    return joined(jnp.dot(left, right, preferred_element_type=F32))


PARTS = 4


def hand_out(top_in, result_in, top_out, result_out, top_sem, result_sem):
    copies = []
    for source, target, sems in ((result_in, result_out, result_sem), (top_in, top_out, top_sem)):
        rows = source.shape[0] // PARTS
        for part in range(PARTS):
            cut = pl.ds(part * rows, rows)
            copies.append(pltpu.make_async_copy(source.at[cut], target.at[cut], sems.at[part]))
    for copy in copies:
        copy.start()
    for copy in copies:
        copy.wait()


def kernel(
    owners, steps, chunks,
    pivot_hbm, sect_hbm, y_hbm, t_hbm, route_hbm, v_hbm, f_hbm,
    top_hbm, out_hbm,
    top_ref, out_ref,
    pivot_ref, sect_ref, y_ref, t_ref, route_ref, v_ref, f_ref, yt, tt,
    place, slot_row, pivots, pivots_out, contrib, send, arrived, arrived_cat,
    vt, ft, part, part_near, pair, pair_far, total,
    load_sem, top_sem, out_sem, chain_send, chain_recv, swap_send, swap_recv, sum_send, sum_recv,
):
    front = lax.axis_index("front")
    me = lax.axis_index("sect")
    rows = sect_ref.shape[1]
    row_count = sect_ref.shape[0] * rows
    slots = v_ref.shape[0]
    capacity = slots // owners
    depth = pivot_ref.shape[0]
    half = depth // 2
    odd = lax.rem(me, 2)
    near = me + 1 - 2 * odd
    far = me + 2 - 4 * lax.rem(me // 2, 2)
    right = lax.rem(me + 1, steps)

    def peer(m):
        found = 0
        bit = 1
        while bit < owners:
            found = found + bit * lax.rem(front // bit + m // bit, 2)
            bit *= 2
        return found

    def panel_of(step):
        return lax.rem(me - step + steps, steps)

    def panel_loads(step):
        panel = panel_of(step)
        pairs = ((sect_hbm, sect_ref), (y_hbm, y_ref), (t_hbm, t_ref))
        return [
            pltpu.make_async_copy(source.at[panel], target.at[panel], load_sem.at[3 * step + i])
            for i, (source, target) in enumerate(pairs)
        ]

    def whole_load(index):
        source, target = (
            (pivot_hbm, pivot_ref), (route_hbm, route_ref), (v_hbm, v_ref), (f_hbm, f_ref)
        )[index]
        return pltpu.make_async_copy(source, target, load_sem.at[3 * steps + index])

    for copy in [whole_load(0)] + panel_loads(0) + [whole_load(1)]:
        copy.start()
    for step in range(1, steps):
        for copy in panel_loads(step):
            copy.start()
    whole_load(2).start()
    whole_load(3).start()

    barrier = pltpu.get_barrier_semaphore()

    @pl.loop(1, owners)
    def _(m):
        pl.semaphore_signal(barrier, inc=1, device_id={"front": peer(m)}, device_id_type=MESH)

    for shift in range(1, steps):
        pl.semaphore_signal(
            barrier, inc=1, device_id={"sect": lax.rem(me + shift, steps)}, device_id_type=MESH
        )

    def columns(chunk):
        if isinstance(chunk, int):
            return pl.ds(chunk * WIDTH, WIDTH)
        return pl.ds(pl.multiple_of(chunk * WIDTH, WIDTH), WIDTH)

    def chain_copy(chunk, step):
        return pltpu.make_async_remote_copy(
            src_ref=pivots_out.at[chunk * steps + step],
            dst_ref=pivots.at[chunk * steps + step],
            send_sem=chain_send.at[chunk * steps + step],
            recv_sem=chain_recv.at[chunk * steps + step],
            device_id={"sect": right},
            device_id_type=MESH,
        )

    def swap_copy(chunk, m):
        to = peer(m)
        return pltpu.make_async_remote_copy(
            src_ref=send.at[chunk, pl.ds(pl.multiple_of(to * capacity, 8), capacity)],
            dst_ref=arrived.at[chunk, pl.ds(pl.multiple_of(front * capacity, 8), capacity)],
            send_sem=swap_send.at[chunk],
            recv_sem=swap_recv.at[chunk],
            device_id={"front": to},
            device_id_type=MESH,
        )

    def build_place():
        whole_load(1).wait()
        lanes = 128
        before = (
            lax.broadcasted_iota(jnp.int32, (lanes, lanes), 0)
            <= lax.broadcasted_iota(jnp.int32, (lanes, lanes), 1)
        ).astype(F32)
        owner_ids = lax.broadcasted_iota(jnp.int32, (owners, lanes), 0)
        carry = jnp.zeros((owners, 1), F32)
        for group in range(row_count // lanes):
            cut = slice(group * lanes, (group + 1) * lanes)
            named = route_ref[:, cut]
            hit = (owner_ids == named).astype(F32)
            count = jnp.dot(hit, before, preferred_element_type=F32) + carry
            rank = jnp.sum(hit * count, axis=0, keepdims=True) - 1.0
            slot_row[:, cut] = named.astype(F32) * float(capacity) + rank
            carry = carry + jnp.sum(hit, axis=1, keepdims=True)

        @pl.loop(0, slots // TILE)
        def _(tile):
            ids = lax.broadcasted_iota(jnp.int32, (TILE, row_count), 0) + tile * TILE
            hit = ids.astype(F32) == slot_row[...]
            place[pl.ds(pl.multiple_of(tile * TILE, TILE), TILE), :] = hit.astype(F32).astype(BF16)

    def reflect(chunk, step):
        panel = panel_of(step)
        row_block = sect_ref[panel, :, columns(chunk)]
        projected = dot(yt[panel], halves(row_block))
        if step == 0:
            pivot_block = pivot_ref[:, columns(chunk)]
        else:
            chain_copy(chunk, step - 1).wait_recv()
            pivot_block = pivots[chunk * steps + step - 1]
        change = dot(tt[panel], halves(pivot_block + projected))
        pivots_out[chunk * steps + step] = pivot_block - change
        if step == 0 and isinstance(chunk, int):
            pl.semaphore_wait(barrier, owners - 1 + steps - 1)
        chain_copy(chunk, step).start()
        updated = row_block - dot(y_ref[panel], halves(change))
        contrib[chunk, pl.ds(pl.multiple_of(panel * rows, rows), rows), :] = halves(updated)

    def exchange(chunk):
        @pl.loop(0, slots // TILE)
        def _(tile):
            cut = pl.ds(pl.multiple_of(tile * TILE, TILE), TILE)
            send[chunk, cut, :] = dot(place[cut, :], contrib[chunk])

        @pl.loop(1, owners)
        def _(m):
            swap_copy(chunk, owners - m).start()

        own = pl.ds(pl.multiple_of(front * capacity, 8), capacity)
        arrived[chunk, own, :] = send[chunk, own, :]

    whole_load(0).wait()
    for step in range(steps):
        for copy in panel_loads(step):
            copy.wait()
        panel = panel_of(step)
        yt[panel] = y_ref[panel].T
        tt[panel] = t_ref[panel].T
        reflect(0, step)
        if step == 0:
            build_place()
    exchange(0)

    @pl.loop(1, chunks)
    def _(chunk):
        for step in range(steps):
            reflect(chunk, step)
        exchange(chunk)

    whole_load(2).wait()
    whole_load(3).wait()

    @pl.loop(0, slots // TILE)
    def _(tile):
        cut = pl.ds(pl.multiple_of(tile * TILE, TILE), TILE)
        vt[:, cut] = v_ref[cut, :].T

    ft[...] = f_ref[...].T

    @pl.loop(0, chunks)
    def _(chunk):
        chain_copy(chunk, steps - 1).wait_recv()
        top_ref[:, columns(chunk)] = pivots[chunk * steps + steps - 1]

    top_copy = pltpu.make_async_copy(top_ref, top_hbm, top_sem)
    top_copy.start()

    def out_copy(chunk):
        cut = columns(chunk)
        return pltpu.make_async_copy(out_ref.at[:, cut], out_hbm.at[:, cut], out_sem.at[chunk])

    def sum_copy(chunk, stage, source, target, to):
        return pltpu.make_async_remote_copy(
            src_ref=source,
            dst_ref=target,
            send_sem=sum_send.at[chunk * 3 + stage],
            recv_sem=sum_recv.at[chunk * 3 + stage],
            device_id={"sect": to},
            device_id_type=MESH,
        )

    mine = pl.ds(pl.multiple_of(odd * half, half), half)
    other = pl.ds(pl.multiple_of((1 - odd) * half, half), half)

    def sum_copies(chunk):
        return (
            sum_copy(chunk, 0, part.at[chunk, other], part_near.at[chunk], near),
            sum_copy(chunk, 1, pair.at[chunk], pair_far.at[chunk], far),
            sum_copy(chunk, 2, total.at[chunk, mine], total.at[chunk, mine], near),
        )

    def swapped(chunk, sem):
        whole = send.at[chunk, pl.ds(0, (owners - 1) * capacity)]
        return pltpu.make_async_copy(whole, whole, sem.at[chunk])

    @pl.loop(0, chunks)
    def _(chunk):
        swapped(chunk, swap_recv).wait()
        first, second, third = sum_copies(chunk)

        @pl.loop(0, slots // TILE)
        def _(tile):
            cut = pl.ds(pl.multiple_of(tile * TILE, TILE), TILE)
            arrived_cat[cut, :] = halves(arrived[chunk, cut, :])

        part[chunk, other, :] = dot(vt[other, :], arrived_cat[...])
        first.start()
        part[chunk, mine, :] = dot(vt[mine, :], arrived_cat[...])
        first.wait_recv()
        pair[chunk] = part[chunk, mine, :] + part_near[chunk]
        second.start()
        second.wait_recv()
        total[chunk, mine, :] = pair[chunk] + pair_far[chunk]
        third.start()
        third.wait_recv()
        change = halves(dot(ft[...], halves(total[chunk])))

        @pl.loop(0, slots // TILE)
        def _(tile):
            cut = pl.ds(pl.multiple_of(tile * TILE, TILE), TILE)
            out_ref[cut, columns(chunk)] = arrived[chunk, cut, :] - dot(v_ref[cut, :], change)

        out_copy(chunk).start()

    @pl.loop(0, chunks)
    def _(chunk):
        for copy in sum_copies(chunk):
            copy.wait_send()
        out_copy(chunk).wait()
        swapped(chunk, swap_send).wait()

    @pl.loop(0, chunks * steps)
    def _(index):
        chain_copy(index // steps, lax.rem(index, steps)).wait_send()

    top_copy.wait()


def local(pivot_rows, sections, sect_vectors, sect_factors, routes, parent_vectors, parent_factor):
    owners = lax.axis_size("front")
    steps = lax.axis_size("sect")
    panels, rows, columns = sections.shape[2:]
    depth = pivot_rows.shape[2]
    slots = parent_vectors.shape[2]
    row_count = panels * rows
    chunks = columns // WIDTH
    half = depth // 2
    hbm = pl.BlockSpec(memory_space=pltpu.HBM)
    dma = pltpu.SemaphoreType.DMA
    top, result = pl.pallas_call(
        functools.partial(kernel, owners, steps, chunks),
        out_shape=(
            jax.ShapeDtypeStruct((depth, columns), F32),
            jax.ShapeDtypeStruct((slots, columns), F32),
        ),
        in_specs=[hbm] * 7,
        out_specs=(hbm, hbm),
        scratch_shapes=[
            pltpu.VMEM((depth, columns), F32),
            pltpu.VMEM((slots, columns), F32),
            pltpu.VMEM((depth, columns), F32),
            pltpu.VMEM((panels, rows, columns), F32),
            pltpu.VMEM((panels, rows, depth), BF16),
            pltpu.VMEM((panels, depth, depth), BF16),
            pltpu.VMEM((1, row_count), jnp.int32),
            pltpu.VMEM((slots, depth), BF16),
            pltpu.VMEM((depth, depth), BF16),
            pltpu.VMEM((panels, depth, rows), BF16),
            pltpu.VMEM((panels, depth, depth), BF16),
            pltpu.VMEM((slots, row_count), BF16),
            pltpu.VMEM((1, row_count), F32),
            pltpu.VMEM((chunks * steps, depth, WIDTH), F32),
            pltpu.VMEM((chunks * steps, depth, WIDTH), F32),
            pltpu.VMEM((chunks, row_count, 2 * WIDTH), BF16),
            pltpu.VMEM((chunks, slots, WIDTH), F32),
            pltpu.VMEM((chunks, slots, WIDTH), F32),
            pltpu.VMEM((slots, 2 * WIDTH), BF16),
            pltpu.VMEM((depth, slots), BF16),
            pltpu.VMEM((depth, depth), BF16),
            pltpu.VMEM((chunks, depth, WIDTH), F32),
            pltpu.VMEM((chunks, half, WIDTH), F32),
            pltpu.VMEM((chunks, half, WIDTH), F32),
            pltpu.VMEM((chunks, half, WIDTH), F32),
            pltpu.VMEM((chunks, depth, WIDTH), F32),
            dma((3 * steps + 4,)),
            dma,
            dma((chunks,)),
            dma((chunks * steps,)),
            dma((chunks * steps,)),
            dma((chunks,)),
            dma((chunks,)),
            dma((chunks * 3,)),
            dma((chunks * 3,)),
        ],
        compiler_params=pltpu.CompilerParams(
            collective_id=0, has_side_effects=True, vmem_limit_bytes=62 * 2**20
        ),
        cost_estimate=pl.CostEstimate(
            flops=8 * 10**9, bytes_accessed=12 * 2**20, transcendentals=0
        ),
    )(
        pivot_rows[0, 0],
        sections[0, 0],
        sect_vectors[0, 0],
        sect_factors[0, 0],
        routes[0, 0].reshape(1, row_count),
        parent_vectors[0, 0],
        parent_factor[0],
    )
    top, result = pl.pallas_call(
        hand_out,
        out_shape=(
            jax.ShapeDtypeStruct((depth, columns), F32),
            jax.ShapeDtypeStruct((slots, columns), F32),
        ),
        in_specs=[hbm] * 2,
        out_specs=(hbm, hbm),
        scratch_shapes=[dma((PARTS,)), dma((PARTS,))],
        compiler_params=pltpu.CompilerParams(vmem_limit_bytes=62 * 2**20),
        cost_estimate=pl.CostEstimate(flops=0, bytes_accessed=8 * 2**20, transcendentals=0),
    )(top, result)
    return (top[None, None], result[None, None])


def solution(mesh):
    in_specs = (
        P("front", "sect", None, None),
        P("front", "sect", None, None, None),
        P("front", "sect", None, None, None),
        P("front", "sect", None, None, None),
        P("front", "sect", None, None),
        P("front", "sect", None, None),
        P("front", None, None),
    )
    out_specs = (P("front", "sect", None, None), P("front", "sect", None, None))
    return jax.shard_map(local, mesh=mesh, in_specs=in_specs, out_specs=out_specs, check_vma=False)
```

```python
import functools

import jax
import jax.numpy as jnp
from jax import lax
from jax.experimental import pallas as pl
from jax.experimental.pallas import tpu as pltpu
from jax.sharding import PartitionSpec as P

MESH = pl.DeviceIdType.MESH
WIDTH = 128
TILE = 256
F32 = jnp.float32
BF16 = jnp.bfloat16


def halves(value):
    high = value.astype(BF16)
    low = (value - high.astype(F32)).astype(BF16)
    return jnp.concatenate([high, low], axis=1)


def joined(value):
    return value[:, :WIDTH] + value[:, WIDTH:]


def dot(left, right):
    return joined(jnp.dot(left, right, preferred_element_type=F32))


PARTS = 4


def hand_out(top_in, result_in, top_out, result_out, top_mid, result_mid, in_sem, out_sem):
    loads, stores = [], []
    for source, held, target in (
        (result_in, result_mid, result_out), (top_in, top_mid, top_out)
    ):
        rows = source.shape[0] // PARTS
        for part in range(PARTS):
            cut = pl.ds(part * rows, rows)
            index = len(loads)
            loads.append(pltpu.make_async_copy(source.at[cut], held.at[cut], in_sem.at[index]))
            stores.append(pltpu.make_async_copy(held.at[cut], target.at[cut], out_sem.at[index]))
    for load in loads:
        load.start()
    for load, store in zip(loads, stores):
        load.wait()
        store.start()
    for store in stores:
        store.wait()


def kernel(
    owners, steps, chunks,
    pivot_hbm, sect_hbm, y_hbm, t_hbm, route_hbm, v_hbm, f_hbm,
    top_hbm, out_hbm,
    top_ref, out_ref,
    pivot_ref, sect_ref, y_ref, t_ref, route_ref, v_ref, f_ref, yt, tt,
    place, slot_row, pivots, pivots_out, contrib, send, arrived, arrived_cat,
    vt, ft, part, part_near, pair, pair_far, total,
    load_sem, top_sem, out_sem, chain_send, chain_recv, swap_send, swap_recv, sum_send, sum_recv,
):
    front = lax.axis_index("front")
    me = lax.axis_index("sect")
    rows = sect_ref.shape[1]
    row_count = sect_ref.shape[0] * rows
    slots = v_ref.shape[0]
    capacity = slots // owners
    depth = pivot_ref.shape[0]
    half = depth // 2
    odd = lax.rem(me, 2)
    near = me + 1 - 2 * odd
    far = me + 2 - 4 * lax.rem(me // 2, 2)
    right = lax.rem(me + 1, steps)

    def peer(m):
        found = 0
        bit = 1
        while bit < owners:
            found = found + bit * lax.rem(front // bit + m // bit, 2)
            bit *= 2
        return found

    def panel_of(step):
        return lax.rem(me - step + steps, steps)

    def panel_loads(step):
        panel = panel_of(step)
        pairs = ((sect_hbm, sect_ref), (y_hbm, y_ref), (t_hbm, t_ref))
        return [
            pltpu.make_async_copy(source.at[panel], target.at[panel], load_sem.at[3 * step + i])
            for i, (source, target) in enumerate(pairs)
        ]

    def whole_load(index):
        source, target = (
            (pivot_hbm, pivot_ref), (route_hbm, route_ref), (v_hbm, v_ref), (f_hbm, f_ref)
        )[index]
        return pltpu.make_async_copy(source, target, load_sem.at[3 * steps + index])

    for copy in [whole_load(0)] + panel_loads(0) + [whole_load(1)]:
        copy.start()
    for step in range(1, steps):
        for copy in panel_loads(step):
            copy.start()
    whole_load(2).start()
    whole_load(3).start()

    barrier = pltpu.get_barrier_semaphore()

    @pl.loop(1, owners)
    def _(m):
        pl.semaphore_signal(barrier, inc=1, device_id={"front": peer(m)}, device_id_type=MESH)

    for shift in range(1, steps):
        pl.semaphore_signal(
            barrier, inc=1, device_id={"sect": lax.rem(me + shift, steps)}, device_id_type=MESH
        )

    def columns(chunk):
        if isinstance(chunk, int):
            return pl.ds(chunk * WIDTH, WIDTH)
        return pl.ds(pl.multiple_of(chunk * WIDTH, WIDTH), WIDTH)

    def chain_copy(chunk, step):
        return pltpu.make_async_remote_copy(
            src_ref=pivots_out.at[chunk * steps + step],
            dst_ref=pivots.at[chunk * steps + step],
            send_sem=chain_send.at[chunk * steps + step],
            recv_sem=chain_recv.at[chunk * steps + step],
            device_id={"sect": right},
            device_id_type=MESH,
        )

    def swap_copy(chunk, m):
        to = peer(m)
        return pltpu.make_async_remote_copy(
            src_ref=send.at[chunk, pl.ds(pl.multiple_of(to * capacity, 8), capacity)],
            dst_ref=arrived.at[chunk, pl.ds(pl.multiple_of(front * capacity, 8), capacity)],
            send_sem=swap_send.at[chunk],
            recv_sem=swap_recv.at[chunk],
            device_id={"front": to},
            device_id_type=MESH,
        )

    def build_place():
        whole_load(1).wait()
        lanes = 128
        before = (
            lax.broadcasted_iota(jnp.int32, (lanes, lanes), 0)
            <= lax.broadcasted_iota(jnp.int32, (lanes, lanes), 1)
        ).astype(F32)
        owner_ids = lax.broadcasted_iota(jnp.int32, (owners, lanes), 0)
        carry = jnp.zeros((owners, 1), F32)
        for group in range(row_count // lanes):
            cut = slice(group * lanes, (group + 1) * lanes)
            named = route_ref[:, cut]
            hit = (owner_ids == named).astype(F32)
            count = jnp.dot(hit, before, preferred_element_type=F32) + carry
            rank = jnp.sum(hit * count, axis=0, keepdims=True) - 1.0
            slot_row[:, cut] = named.astype(F32) * float(capacity) + rank
            carry = carry + jnp.sum(hit, axis=1, keepdims=True)

        @pl.loop(0, slots // TILE)
        def _(tile):
            ids = lax.broadcasted_iota(jnp.int32, (TILE, row_count), 0) + tile * TILE
            hit = ids.astype(F32) == slot_row[...]
            place[pl.ds(pl.multiple_of(tile * TILE, TILE), TILE), :] = hit.astype(F32).astype(BF16)

    def reflect(chunk, step):
        panel = panel_of(step)
        row_block = sect_ref[panel, :, columns(chunk)]
        projected = dot(yt[panel], halves(row_block))
        if step == 0:
            pivot_block = pivot_ref[:, columns(chunk)]
        else:
            chain_copy(chunk, step - 1).wait_recv()
            pivot_block = pivots[chunk * steps + step - 1]
        change = dot(tt[panel], halves(pivot_block + projected))
        pivots_out[chunk * steps + step] = pivot_block - change
        if step == 0 and isinstance(chunk, int) and chunk == 0:
            pl.semaphore_wait(barrier, owners - 1 + steps - 1)
        chain_copy(chunk, step).start()
        updated = row_block - dot(y_ref[panel], halves(change))
        contrib[chunk, pl.ds(pl.multiple_of(panel * rows, rows), rows), :] = halves(updated)

    def exchange(chunk):
        @pl.loop(0, slots // TILE)
        def _(tile):
            cut = pl.ds(pl.multiple_of(tile * TILE, TILE), TILE)
            send[chunk, cut, :] = dot(place[cut, :], contrib[chunk])

        @pl.loop(0, owners - 1)
        def _(turn):
            m = 1 + lax.rem((owners // 2 - 1) * (turn + 1) + 2 * odd, owners - 1)
            swap_copy(chunk, m).start()

        own = pl.ds(pl.multiple_of(front * capacity, 8), capacity)
        arrived[chunk, own, :] = send[chunk, own, :]

    whole_load(0).wait()
    for step in range(steps):
        for copy in panel_loads(step):
            copy.wait()
        panel = panel_of(step)
        yt[panel] = y_ref[panel].T
        tt[panel] = t_ref[panel].T
        if step == steps - 1 and chunks > 1:
            reflect(1, 0)
        reflect(0, step)
        if step == 0:
            build_place()
    exchange(0)

    @pl.loop(1, chunks)
    def _(chunk):
        for step in range(1, steps - 1):
            reflect(chunk, step)

        @pl.when(chunk + 1 < chunks)
        def _():
            reflect(chunk + 1, 0)

        reflect(chunk, steps - 1)
        exchange(chunk)

    whole_load(2).wait()
    whole_load(3).wait()

    @pl.loop(0, slots // TILE)
    def _(tile):
        cut = pl.ds(pl.multiple_of(tile * TILE, TILE), TILE)
        vt[:, cut] = v_ref[cut, :].T

    ft[...] = f_ref[...].T

    @pl.loop(0, chunks)
    def _(chunk):
        chain_copy(chunk, steps - 1).wait_recv()
        top_ref[:, columns(chunk)] = pivots[chunk * steps + steps - 1]

    top_copy = pltpu.make_async_copy(top_ref, top_hbm, top_sem)
    top_copy.start()

    def out_copy(chunk):
        cut = columns(chunk)
        return pltpu.make_async_copy(out_ref.at[:, cut], out_hbm.at[:, cut], out_sem.at[chunk])

    def sum_copy(chunk, stage, source, target, to):
        return pltpu.make_async_remote_copy(
            src_ref=source,
            dst_ref=target,
            send_sem=sum_send.at[chunk * 3 + stage],
            recv_sem=sum_recv.at[chunk * 3 + stage],
            device_id={"sect": to},
            device_id_type=MESH,
        )

    mine = pl.ds(pl.multiple_of(odd * half, half), half)
    other = pl.ds(pl.multiple_of((1 - odd) * half, half), half)

    def sum_copies(chunk):
        return (
            sum_copy(chunk, 0, part.at[chunk, other], part_near.at[chunk], near),
            sum_copy(chunk, 1, pair.at[chunk], pair_far.at[chunk], far),
            sum_copy(chunk, 2, total.at[chunk, mine], total.at[chunk, mine], near),
        )

    def swapped(chunk, sem):
        whole = send.at[chunk, pl.ds(0, (owners - 1) * capacity)]
        return pltpu.make_async_copy(whole, whole, sem.at[chunk])

    @pl.loop(0, chunks)
    def _(chunk):
        swapped(chunk, swap_recv).wait()
        first, second, third = sum_copies(chunk)

        @pl.loop(0, slots // TILE)
        def _(tile):
            cut = pl.ds(pl.multiple_of(tile * TILE, TILE), TILE)
            arrived_cat[cut, :] = halves(arrived[chunk, cut, :])

        part[chunk, other, :] = dot(vt[other, :], arrived_cat[...])
        first.start()
        part[chunk, mine, :] = dot(vt[mine, :], arrived_cat[...])
        first.wait_recv()
        pair[chunk] = part[chunk, mine, :] + part_near[chunk]
        second.start()
        second.wait_recv()
        total[chunk, mine, :] = pair[chunk] + pair_far[chunk]
        third.start()
        third.wait_recv()
        change = halves(dot(ft[...], halves(total[chunk])))

        @pl.loop(0, slots // TILE)
        def _(tile):
            cut = pl.ds(pl.multiple_of(tile * TILE, TILE), TILE)
            out_ref[cut, columns(chunk)] = arrived[chunk, cut, :] - dot(v_ref[cut, :], change)

        out_copy(chunk).start()

    @pl.loop(0, chunks)
    def _(chunk):
        for copy in sum_copies(chunk):
            copy.wait_send()
        out_copy(chunk).wait()
        swapped(chunk, swap_send).wait()

    @pl.loop(0, chunks * steps)
    def _(index):
        chain_copy(index // steps, lax.rem(index, steps)).wait_send()

    top_copy.wait()


def local(pivot_rows, sections, sect_vectors, sect_factors, routes, parent_vectors, parent_factor):
    owners = lax.axis_size("front")
    steps = lax.axis_size("sect")
    panels, rows, columns = sections.shape[2:]
    depth = pivot_rows.shape[2]
    slots = parent_vectors.shape[2]
    row_count = panels * rows
    chunks = columns // WIDTH
    half = depth // 2
    hbm = pl.BlockSpec(memory_space=pltpu.HBM)
    dma = pltpu.SemaphoreType.DMA
    top, result = pl.pallas_call(
        functools.partial(kernel, owners, steps, chunks),
        out_shape=(
            jax.ShapeDtypeStruct((depth, columns), F32),
            jax.ShapeDtypeStruct((slots, columns), F32),
        ),
        in_specs=[hbm] * 7,
        out_specs=(hbm, hbm),
        scratch_shapes=[
            pltpu.VMEM((depth, columns), F32),
            pltpu.VMEM((slots, columns), F32),
            pltpu.VMEM((depth, columns), F32),
            pltpu.VMEM((panels, rows, columns), F32),
            pltpu.VMEM((panels, rows, depth), BF16),
            pltpu.VMEM((panels, depth, depth), BF16),
            pltpu.VMEM((1, row_count), jnp.int32),
            pltpu.VMEM((slots, depth), BF16),
            pltpu.VMEM((depth, depth), BF16),
            pltpu.VMEM((panels, depth, rows), BF16),
            pltpu.VMEM((panels, depth, depth), BF16),
            pltpu.VMEM((slots, row_count), BF16),
            pltpu.VMEM((1, row_count), F32),
            pltpu.VMEM((chunks * steps, depth, WIDTH), F32),
            pltpu.VMEM((chunks * steps, depth, WIDTH), F32),
            pltpu.VMEM((chunks, row_count, 2 * WIDTH), BF16),
            pltpu.VMEM((chunks, slots, WIDTH), F32),
            pltpu.VMEM((chunks, slots, WIDTH), F32),
            pltpu.VMEM((slots, 2 * WIDTH), BF16),
            pltpu.VMEM((depth, slots), BF16),
            pltpu.VMEM((depth, depth), BF16),
            pltpu.VMEM((chunks, depth, WIDTH), F32),
            pltpu.VMEM((chunks, half, WIDTH), F32),
            pltpu.VMEM((chunks, half, WIDTH), F32),
            pltpu.VMEM((chunks, half, WIDTH), F32),
            pltpu.VMEM((chunks, depth, WIDTH), F32),
            dma((3 * steps + 4,)),
            dma,
            dma((chunks,)),
            dma((chunks * steps,)),
            dma((chunks * steps,)),
            dma((chunks,)),
            dma((chunks,)),
            dma((chunks * 3,)),
            dma((chunks * 3,)),
        ],
        compiler_params=pltpu.CompilerParams(
            collective_id=0, has_side_effects=True, vmem_limit_bytes=62 * 2**20
        ),
        cost_estimate=pl.CostEstimate(
            flops=8 * 10**9, bytes_accessed=12 * 2**20, transcendentals=0
        ),
    )(
        pivot_rows[0, 0],
        sections[0, 0],
        sect_vectors[0, 0],
        sect_factors[0, 0],
        routes[0, 0].reshape(1, row_count),
        parent_vectors[0, 0],
        parent_factor[0],
    )
    top, result = pl.pallas_call(
        hand_out,
        out_shape=(
            jax.ShapeDtypeStruct((depth, columns), F32),
            jax.ShapeDtypeStruct((slots, columns), F32),
        ),
        in_specs=[hbm] * 2,
        out_specs=(hbm, hbm),
        scratch_shapes=[
            pltpu.VMEM((depth, columns), F32),
            pltpu.VMEM((slots, columns), F32),
            dma((2 * PARTS,)),
            dma((2 * PARTS,)),
        ],
        compiler_params=pltpu.CompilerParams(vmem_limit_bytes=62 * 2**20),
        cost_estimate=pl.CostEstimate(flops=0, bytes_accessed=8 * 2**20, transcendentals=0),
    )(top, result)
    return (top[None, None], result[None, None])


def solution(mesh):
    in_specs = (
        P("front", "sect", None, None),
        P("front", "sect", None, None, None),
        P("front", "sect", None, None, None),
        P("front", "sect", None, None, None),
        P("front", "sect", None, None),
        P("front", "sect", None, None),
        P("front", None, None),
    )
    out_specs = (P("front", "sect", None, None), P("front", "sect", None, None))
    return jax.shard_map(local, mesh=mesh, in_specs=in_specs, out_specs=out_specs, check_vma=False)
```

```python
import functools

import jax
import jax.numpy as jnp
from jax import lax
from jax.experimental import pallas as pl
from jax.experimental.pallas import tpu as pltpu
from jax.sharding import PartitionSpec as P

MESH = pl.DeviceIdType.MESH
WIDTH = 128
TILE = 256
F32 = jnp.float32
BF16 = jnp.bfloat16


def halves(value):
    high = value.astype(BF16)
    low = (value - high.astype(F32)).astype(BF16)
    return jnp.concatenate([high, low], axis=1)


def joined(value):
    return value[:, :WIDTH] + value[:, WIDTH:]


def dot(left, right):
    return joined(jnp.dot(left, right, preferred_element_type=F32))


PARTS = 4


def hand_out(top_in, result_in, top_out, result_out, top_mid, result_mid, in_sem, out_sem):
    loads, stores = [], []
    for source, held, target in (
        (result_in, result_mid, result_out), (top_in, top_mid, top_out)
    ):
        rows = source.shape[0] // PARTS
        for part in range(PARTS):
            cut = pl.ds(part * rows, rows)
            index = len(loads)
            loads.append(pltpu.make_async_copy(source.at[cut], held.at[cut], in_sem.at[index]))
            stores.append(pltpu.make_async_copy(held.at[cut], target.at[cut], out_sem.at[index]))
    for load in loads:
        load.start()
    for load, store in zip(loads, stores):
        load.wait()
        store.start()
    for store in stores:
        store.wait()


def kernel(
    owners, steps, chunks,
    pivot_hbm, sect_hbm, y_hbm, t_hbm, route_hbm, v_hbm, f_hbm,
    top_hbm, out_hbm,
    top_ref, out_ref,
    pivot_ref, sect_ref, y_ref, t_ref, route_ref, v_ref, f_ref, yt, tt,
    place, slot_row, pivots, pivots_out, contrib, send, arrived, arrived_cat,
    vt, ft, part, part_near, pair, pair_far, total,
    load_sem, top_sem, out_sem, chain_send, chain_recv, swap_send, swap_recv, sum_send, sum_recv,
):
    front = lax.axis_index("front")
    me = lax.axis_index("sect")
    rows = sect_ref.shape[1]
    row_count = sect_ref.shape[0] * rows
    slots = v_ref.shape[0]
    capacity = slots // owners
    depth = pivot_ref.shape[0]
    half = depth // 2
    odd = lax.rem(me, 2)
    near = me + 1 - 2 * odd
    far = me + 2 - 4 * lax.rem(me // 2, 2)
    right = lax.rem(me + 1, steps)
    middle = lax.rem(front // (owners // 2) + front // (owners // 4), 2)

    def peer(m):
        found = 0
        bit = 1
        while bit < owners:
            found = found + bit * lax.rem(front // bit + m // bit, 2)
            bit *= 2
        return found

    def panel_of(step):
        return lax.rem(me - step + steps, steps)

    def panel_loads(step):
        panel = panel_of(step)
        pairs = ((sect_hbm, sect_ref), (y_hbm, y_ref), (t_hbm, t_ref))
        return [
            pltpu.make_async_copy(source.at[panel], target.at[panel], load_sem.at[3 * step + i])
            for i, (source, target) in enumerate(pairs)
        ]

    def whole_load(index):
        source, target = (
            (pivot_hbm, pivot_ref), (route_hbm, route_ref), (v_hbm, v_ref), (f_hbm, f_ref)
        )[index]
        return pltpu.make_async_copy(source, target, load_sem.at[3 * steps + index])

    for copy in [whole_load(0)] + panel_loads(0) + [whole_load(1)]:
        copy.start()
    for step in range(1, steps):
        for copy in panel_loads(step):
            copy.start()
    whole_load(2).start()
    whole_load(3).start()

    barrier = pltpu.get_barrier_semaphore()

    @pl.loop(1, owners)
    def _(m):
        pl.semaphore_signal(barrier, inc=1, device_id={"front": peer(m)}, device_id_type=MESH)

    for shift in range(1, steps):
        pl.semaphore_signal(
            barrier, inc=1, device_id={"sect": lax.rem(me + shift, steps)}, device_id_type=MESH
        )

    def columns(chunk):
        if isinstance(chunk, int):
            return pl.ds(chunk * WIDTH, WIDTH)
        return pl.ds(pl.multiple_of(chunk * WIDTH, WIDTH), WIDTH)

    def chain_copy(chunk, step):
        return pltpu.make_async_remote_copy(
            src_ref=pivots_out.at[chunk * steps + step],
            dst_ref=pivots.at[chunk * steps + step],
            send_sem=chain_send.at[chunk * steps + step],
            recv_sem=chain_recv.at[chunk * steps + step],
            device_id={"sect": right},
            device_id_type=MESH,
        )

    def swap_copy(chunk, m):
        to = peer(m)
        return pltpu.make_async_remote_copy(
            src_ref=send.at[chunk, pl.ds(pl.multiple_of(to * capacity, 8), capacity)],
            dst_ref=arrived.at[chunk, pl.ds(pl.multiple_of(front * capacity, 8), capacity)],
            send_sem=swap_send.at[chunk],
            recv_sem=swap_recv.at[chunk],
            device_id={"front": to},
            device_id_type=MESH,
        )

    def build_place():
        whole_load(1).wait()
        lanes = 128
        before = (
            lax.broadcasted_iota(jnp.int32, (lanes, lanes), 0)
            <= lax.broadcasted_iota(jnp.int32, (lanes, lanes), 1)
        ).astype(F32)
        owner_ids = lax.broadcasted_iota(jnp.int32, (owners, lanes), 0)
        carry = jnp.zeros((owners, 1), F32)
        for group in range(row_count // lanes):
            cut = slice(group * lanes, (group + 1) * lanes)
            named = route_ref[:, cut]
            hit = (owner_ids == named).astype(F32)
            count = jnp.dot(hit, before, preferred_element_type=F32) + carry
            rank = jnp.sum(hit * count, axis=0, keepdims=True) - 1.0
            slot_row[:, cut] = named.astype(F32) * float(capacity) + rank
            carry = carry + jnp.sum(hit, axis=1, keepdims=True)

        @pl.loop(0, slots // TILE)
        def _(tile):
            ids = lax.broadcasted_iota(jnp.int32, (TILE, row_count), 0) + tile * TILE
            hit = ids.astype(F32) == slot_row[...]
            place[pl.ds(pl.multiple_of(tile * TILE, TILE), TILE), :] = hit.astype(F32).astype(BF16)

    def reflect(chunk, step):
        panel = panel_of(step)
        row_block = sect_ref[panel, :, columns(chunk)]
        projected = dot(yt[panel], halves(row_block))
        if step == 0:
            pivot_block = pivot_ref[:, columns(chunk)]
        else:
            chain_copy(chunk, step - 1).wait_recv()
            pivot_block = pivots[chunk * steps + step - 1]
        change = dot(tt[panel], halves(pivot_block + projected))
        pivots_out[chunk * steps + step] = pivot_block - change
        if step == 0 and isinstance(chunk, int) and chunk == 0:
            pl.semaphore_wait(barrier, owners - 1 + steps - 1)
        chain_copy(chunk, step).start()
        updated = row_block - dot(y_ref[panel], halves(change))
        contrib[chunk, pl.ds(pl.multiple_of(panel * rows, rows), rows), :] = halves(updated)

    def exchange(chunk):
        @pl.loop(0, slots // TILE)
        def _(tile):
            cut = pl.ds(pl.multiple_of(tile * TILE, TILE), TILE)
            send[chunk, cut, :] = dot(place[cut, :], contrib[chunk])

        @pl.loop(1, owners)
        def _(turn):
            i = owners - turn
            upper = i // (owners // 2)
            lower = lax.rem(i // (owners // 4), 2) * (1 - upper)
            m = i + middle * ((owners // 2) * lower - (owners // 4) * upper)
            swap_copy(chunk, m).start()

        own = pl.ds(pl.multiple_of(front * capacity, 8), capacity)
        arrived[chunk, own, :] = send[chunk, own, :]

    whole_load(0).wait()
    for step in range(steps):
        for copy in panel_loads(step):
            copy.wait()
        panel = panel_of(step)
        yt[panel] = y_ref[panel].T
        tt[panel] = t_ref[panel].T
        if step == steps - 1 and chunks > 1:
            reflect(1, 0)
        reflect(0, step)
        if step == 0:
            build_place()
    exchange(0)

    @pl.loop(1, chunks)
    def _(chunk):
        for step in range(1, steps - 1):
            reflect(chunk, step)

        @pl.when(chunk + 1 < chunks)
        def _():
            reflect(chunk + 1, 0)

        reflect(chunk, steps - 1)
        exchange(chunk)

    whole_load(2).wait()
    whole_load(3).wait()

    @pl.loop(0, slots // TILE)
    def _(tile):
        cut = pl.ds(pl.multiple_of(tile * TILE, TILE), TILE)
        vt[:, cut] = v_ref[cut, :].T

    ft[...] = f_ref[...].T

    @pl.loop(0, chunks)
    def _(chunk):
        chain_copy(chunk, steps - 1).wait_recv()
        top_ref[:, columns(chunk)] = pivots[chunk * steps + steps - 1]

    top_copy = pltpu.make_async_copy(top_ref, top_hbm, top_sem)
    top_copy.start()

    def out_copy(chunk):
        cut = columns(chunk)
        return pltpu.make_async_copy(out_ref.at[:, cut], out_hbm.at[:, cut], out_sem.at[chunk])

    def sum_copy(chunk, stage, source, target, to):
        return pltpu.make_async_remote_copy(
            src_ref=source,
            dst_ref=target,
            send_sem=sum_send.at[chunk * 3 + stage],
            recv_sem=sum_recv.at[chunk * 3 + stage],
            device_id={"sect": to},
            device_id_type=MESH,
        )

    mine = pl.ds(pl.multiple_of(odd * half, half), half)
    other = pl.ds(pl.multiple_of((1 - odd) * half, half), half)

    def sum_copies(chunk):
        return (
            sum_copy(chunk, 0, part.at[chunk, other], part_near.at[chunk], near),
            sum_copy(chunk, 1, pair.at[chunk], pair_far.at[chunk], far),
            sum_copy(chunk, 2, total.at[chunk, mine], total.at[chunk, mine], near),
        )

    def swapped(chunk, sem):
        whole = send.at[chunk, pl.ds(0, (owners - 1) * capacity)]
        return pltpu.make_async_copy(whole, whole, sem.at[chunk])

    @pl.loop(0, chunks)
    def _(chunk):
        swapped(chunk, swap_recv).wait()
        first, second, third = sum_copies(chunk)

        @pl.loop(0, slots // TILE)
        def _(tile):
            cut = pl.ds(pl.multiple_of(tile * TILE, TILE), TILE)
            arrived_cat[cut, :] = halves(arrived[chunk, cut, :])

        part[chunk, other, :] = dot(vt[other, :], arrived_cat[...])
        first.start()
        part[chunk, mine, :] = dot(vt[mine, :], arrived_cat[...])
        first.wait_recv()
        pair[chunk] = part[chunk, mine, :] + part_near[chunk]
        second.start()
        second.wait_recv()
        total[chunk, mine, :] = pair[chunk] + pair_far[chunk]
        third.start()
        third.wait_recv()
        change = halves(dot(ft[...], halves(total[chunk])))

        @pl.loop(0, slots // TILE)
        def _(tile):
            cut = pl.ds(pl.multiple_of(tile * TILE, TILE), TILE)
            out_ref[cut, columns(chunk)] = arrived[chunk, cut, :] - dot(v_ref[cut, :], change)

        out_copy(chunk).start()

    @pl.loop(0, chunks)
    def _(chunk):
        for copy in sum_copies(chunk):
            copy.wait_send()
        out_copy(chunk).wait()
        swapped(chunk, swap_send).wait()

    @pl.loop(0, chunks * steps)
    def _(index):
        chain_copy(index // steps, lax.rem(index, steps)).wait_send()

    top_copy.wait()


def local(pivot_rows, sections, sect_vectors, sect_factors, routes, parent_vectors, parent_factor):
    owners = lax.axis_size("front")
    steps = lax.axis_size("sect")
    panels, rows, columns = sections.shape[2:]
    depth = pivot_rows.shape[2]
    slots = parent_vectors.shape[2]
    row_count = panels * rows
    chunks = columns // WIDTH
    half = depth // 2
    hbm = pl.BlockSpec(memory_space=pltpu.HBM)
    dma = pltpu.SemaphoreType.DMA
    top, result = pl.pallas_call(
        functools.partial(kernel, owners, steps, chunks),
        out_shape=(
            jax.ShapeDtypeStruct((depth, columns), F32),
            jax.ShapeDtypeStruct((slots, columns), F32),
        ),
        in_specs=[hbm] * 7,
        out_specs=(hbm, hbm),
        scratch_shapes=[
            pltpu.VMEM((depth, columns), F32),
            pltpu.VMEM((slots, columns), F32),
            pltpu.VMEM((depth, columns), F32),
            pltpu.VMEM((panels, rows, columns), F32),
            pltpu.VMEM((panels, rows, depth), BF16),
            pltpu.VMEM((panels, depth, depth), BF16),
            pltpu.VMEM((1, row_count), jnp.int32),
            pltpu.VMEM((slots, depth), BF16),
            pltpu.VMEM((depth, depth), BF16),
            pltpu.VMEM((panels, depth, rows), BF16),
            pltpu.VMEM((panels, depth, depth), BF16),
            pltpu.VMEM((slots, row_count), BF16),
            pltpu.VMEM((1, row_count), F32),
            pltpu.VMEM((chunks * steps, depth, WIDTH), F32),
            pltpu.VMEM((chunks * steps, depth, WIDTH), F32),
            pltpu.VMEM((chunks, row_count, 2 * WIDTH), BF16),
            pltpu.VMEM((chunks, slots, WIDTH), F32),
            pltpu.VMEM((chunks, slots, WIDTH), F32),
            pltpu.VMEM((slots, 2 * WIDTH), BF16),
            pltpu.VMEM((depth, slots), BF16),
            pltpu.VMEM((depth, depth), BF16),
            pltpu.VMEM((chunks, depth, WIDTH), F32),
            pltpu.VMEM((chunks, half, WIDTH), F32),
            pltpu.VMEM((chunks, half, WIDTH), F32),
            pltpu.VMEM((chunks, half, WIDTH), F32),
            pltpu.VMEM((chunks, depth, WIDTH), F32),
            dma((3 * steps + 4,)),
            dma,
            dma((chunks,)),
            dma((chunks * steps,)),
            dma((chunks * steps,)),
            dma((chunks,)),
            dma((chunks,)),
            dma((chunks * 3,)),
            dma((chunks * 3,)),
        ],
        compiler_params=pltpu.CompilerParams(
            collective_id=0, has_side_effects=True, vmem_limit_bytes=62 * 2**20
        ),
        cost_estimate=pl.CostEstimate(
            flops=8 * 10**9, bytes_accessed=12 * 2**20, transcendentals=0
        ),
    )(
        pivot_rows[0, 0],
        sections[0, 0],
        sect_vectors[0, 0],
        sect_factors[0, 0],
        routes[0, 0].reshape(1, row_count),
        parent_vectors[0, 0],
        parent_factor[0],
    )
    top, result = pl.pallas_call(
        hand_out,
        out_shape=(
            jax.ShapeDtypeStruct((depth, columns), F32),
            jax.ShapeDtypeStruct((slots, columns), F32),
        ),
        in_specs=[hbm] * 2,
        out_specs=(hbm, hbm),
        scratch_shapes=[
            pltpu.VMEM((depth, columns), F32),
            pltpu.VMEM((slots, columns), F32),
            dma((2 * PARTS,)),
            dma((2 * PARTS,)),
        ],
        compiler_params=pltpu.CompilerParams(vmem_limit_bytes=62 * 2**20),
        cost_estimate=pl.CostEstimate(flops=0, bytes_accessed=8 * 2**20, transcendentals=0),
    )(top, result)
    return (top[None, None], result[None, None])


def solution(mesh):
    in_specs = (
        P("front", "sect", None, None),
        P("front", "sect", None, None, None),
        P("front", "sect", None, None, None),
        P("front", "sect", None, None, None),
        P("front", "sect", None, None),
        P("front", "sect", None, None),
        P("front", None, None),
    )
    out_specs = (P("front", "sect", None, None), P("front", "sect", None, None))
    return jax.shard_map(local, mesh=mesh, in_specs=in_specs, out_specs=out_specs, check_vma=False)
```
